512 devices in a mesh: pool: 2 (over z_hi), grp: 32 (over x, y, core), tp: 8 (over z_lo).
Axes of the slice: x: 4, y: 4, z: 16 (z_hi: 2, z_lo: 8; z = z_hi * 8 + z_lo), core: 2. Of those that a mesh axis runs over, the one named last changes fastest.
Arguments:
- prompt_states: bfloat16 [32768, 5120], P(('pool', 'grp'), 'tp'), may hold values from -6 to 6
- prompt_lengths: int32 [64, 32], replicated, may hold values from 1 to 16
- prompt_target: int32 [64, 32, 1], replicated, may hold values from 0 to 31; in each aligned block of 32 rows (0 to 31, 32 to 63, ..., all dimensions but the last counted through in order) at most 2 rows name the same one
- prompt_query: bfloat16 [2048, 4, 8192], P(('pool', 'grp'), None, 'tp'), may hold values from -360 to 360
- prompt_next: bfloat16 [2048, 4, 5120], P(('pool', 'grp'), None, 'tp'), may hold values from -6 to 6
- key_weight: bfloat16 [5120, 1024], P(None, 'tp'), may hold values from -0.078125 to 0.078125
- value_weight: bfloat16 [5120, 1024], P(None, 'tp'), may hold values from -0.078125 to 0.078125
- key_gain: float32 [128], replicated, may hold values from 0.1 to 1.9
- seq_query: bfloat16 [256, 4, 8192], P(('pool', 'grp'), None, 'tp'), may hold values from -360 to 360
- seq_next: bfloat16 [256, 4, 5120], P(('pool', 'grp'), None, 'tp'), may hold values from -6 to 6
- cache_kv: bfloat16 [256, 2, 256, 1024], P(('pool', 'grp'), None, None, 'tp'), may hold values from -6 to 6
- context_lengths: int32 [256], P(('pool', 'grp')), may hold values from 1 to 256
Outputs:
- seq_output: bfloat16 [256, 4, 8192], P(('pool', 'grp'), None, 'tp')
- joined_output: bfloat16 [64, 64, 4, 8192], P(('pool', 'grp'), None, None, 'tp')
The draws below stay inside these ranges and needn't reach their ends.
Inputs may be any that keep to these rules, and one draw needn't show every extreme that they name: `prompt_target`: at most 2 prompts of one instance join the same decode instance.
All inputs are finite; a program needn't handle non-finite values.
Results may differ from the reference program's by a relative error of at most 0.011.
Values may be sent and summed in bfloat16 or wider, within the bound.
No kernel may reach another device: no remote copies, remote signals or barrier semaphores. Data moves between devices by JAX's collectives and lax.ppermute only.
A program may use at most 64 MiB of HBM per device.

```python
import math
import jax
import jax.numpy as jnp
import numpy as np
from jax import lax

D = 5120
QH = 64
KVH = 8
HD = 128
QPK = 8
PSLOT = 32
PLEN = 16
SEQ_GRP = 4
CTX = 256
STEPS = 4
MOST = 2
INST = 64
TILE = 512
N_POOL = 2
N_GRP = 32


def scaled_normal(key, shape):
    first_key = jax.random.fold_in(key, 0)
    values = jnp.clip(jax.random.normal(first_key, shape, jnp.float32), -6.0, 6.0)
    return values


def ragged_lengths(key, row_count, column_count, longest):
    first_key, second_key = jax.random.split(key)
    lengths = jax.random.randint(first_key, (row_count, column_count), 1, longest + 1)
    chosen = jax.random.randint(second_key, (row_count, 1), 0, column_count)
    return jnp.where(jnp.arange(column_count)[None, :] == chosen, longest, lengths).astype(jnp.int32)


def draw_prompt_lengths(key, part):
    key = jax.random.fold_in(key, 11)
    return ragged_lengths(key, INST, PSLOT, PLEN)


def draw_context_lengths(key, part):
    key = jax.random.fold_in(key, 13)
    return ragged_lengths(key, INST, SEQ_GRP, CTX).reshape(INST * SEQ_GRP)


def draw_prompt_query(key, part):
    key = jax.random.fold_in(key, 17)
    return scaled_normal(key, (INST * PSLOT, STEPS, QH * HD)).astype(jnp.bfloat16)


def draw_seq_query(key, part):
    key = jax.random.fold_in(key, 19)
    return scaled_normal(key, (INST * SEQ_GRP, STEPS, QH * HD)).astype(jnp.bfloat16)


def shard_levels(own_key, dims, pieces, low, largest):
    gain, own = 1.0, jax.random.fold_in(own_key, 6)
    for dim, blocks in pieces:
        heights = jnp.exp(jax.random.uniform(jax.random.fold_in(own, dim), (blocks,), jnp.float32, low / len(pieces), largest / len(pieces)))
        gain = gain * jnp.repeat(heights, dims[dim] // blocks).reshape([-1 if axis == dim else 1 for axis in range(len(dims))])
    return gain


def assign_block(rng, own, number, rows, count, top, most, lean):
    sequence = jax.random.permutation(rng, count)
    crowded, ordinary = load_shares(count, rows * top, most, lean, True), load_shares(count, rows * top, most, lean, False)
    places = jnp.arange(count)

    def named(sizes, turn):
        used = int((sizes > 0).sum())
        fixed = max(1, used // 4)
        moved = fixed + (places - fixed + turn * (used - fixed)) % max(1, count - fixed)
        return jnp.zeros((count,), jnp.int32).at[sequence[jnp.where(places < fixed, places, moved)]].set(jnp.asarray(sizes, jnp.int32))

    sizes = jnp.where(number % 4 == 0, named(crowded, number // 4), named(ordinary, number - number // 4 - 1))
    mixed = jax.random.permutation(jax.random.fold_in(own, 3), count)
    donor, sink = mixed[0:count // 2 * 2:2], mixed[1:count // 2 * 2:2]
    margin = jnp.minimum(sizes[donor] - 1, most - sizes[sink]) // 2
    margin = jnp.where((donor == sequence[0]) | (sink == sequence[0]) | (sizes[sink] == 0), 0, jnp.maximum(margin, 0))
    moved = jax.random.randint(jax.random.fold_in(own, 4), (count // 2,), 0, 1 << 20) % (margin + 1)
    sizes = sizes.at[donor].add(-moved).at[sink].add(moved)
    items = jnp.searchsorted(jnp.cumsum(sizes), jnp.arange(rows * top), side="right").astype(jnp.int32)
    listing = items.reshape(top, rows).T
    listing = listing[jax.random.permutation(jax.random.fold_in(own, 1), rows)]
    turn = jax.random.randint(jax.random.fold_in(own, 2), (rows, 1), 0, top)
    return jnp.take_along_axis(listing, (jnp.arange(top)[None, :] + turn) % top, axis=1)


def load_shares(number_of, total, bound, lean, full):
    portions = [(1 << 20) // math.isqrt(standing ** lean) + 1 for standing in range(1, number_of + 1)]
    largest = bound if full else min(bound, max(-(-total // number_of), total * portions[0] // sum(portions)))
    least = 1 if total - largest >= number_of - 1 else 0
    counts, surplus = [largest] + [least] * (number_of - 1), total - largest - least * (number_of - 1)
    while surplus > 0:
        candidates = [i for i in range(1, number_of) if counts[i] < largest] or [i for i in range(1, number_of) if counts[i] < bound]
        pool, remaining = sum([portions[i] for i in candidates]), surplus
        for i in candidates:
            more = min(bound - counts[i], max(1, remaining * portions[i] // pool), surplus)
            counts[i] = counts[i] + more
            surplus = surplus - more
    return np.array(counts)


def bell_draw(rng, dims, scale, most, cuts=(), held_as=jnp.bfloat16):
    entries = scale * jax.random.normal(rng, dims, jnp.float32)
    if cuts:
        entries = entries * shard_levels(rng, dims, cuts, -0.22, 0.18)
    return jnp.clip(entries, -most, most).astype(held_as)


def setup_inputs(seed: int = 0) -> dict:
    key_of = jax.random.split(jax.random.key(seed), 13)
    prompt_states = bell_draw(key_of[0], (INST * TILE, D), 1.0, 6.0, ((0, 64), (1, 8)))
    prompt_lengths = draw_prompt_lengths(jax.random.fold_in(key_of[12], 71), 0)
    prompt_target_keys = jax.random.split(jax.random.fold_in(key_of[2], 1), INST * PSLOT // PSLOT)
    prompt_target_turns = jax.random.permutation(jax.random.fold_in(key_of[2], 3), INST * PSLOT // PSLOT)
    prompt_target = jax.vmap(lambda own, number: assign_block(jax.random.fold_in(key_of[2], 2), own, number, PSLOT, N_GRP, 1, MOST, 2))(prompt_target_keys, prompt_target_turns).reshape((INST, PSLOT, 1))
    prompt_query = draw_prompt_query(jax.random.fold_in(key_of[12], 71), 0)
    prompt_next = bell_draw(key_of[4], (INST * PSLOT, STEPS, D), 1.0, 6.0, ((0, 64), (2, 8)))
    key_weight = bell_draw(key_of[5], (D, KVH * HD), D ** -0.5, 0.078125, ((1, 8),))
    value_weight = bell_draw(key_of[6], (D, KVH * HD), D ** -0.5, 0.078125, ((1, 8),))
    key_gain = jnp.clip(1.0 + 0.18 * jax.random.normal(key_of[7], (HD,), jnp.float32), 0.1, 1.9)
    seq_query = draw_seq_query(jax.random.fold_in(key_of[12], 71), 0)
    seq_next = bell_draw(key_of[9], (INST * SEQ_GRP, STEPS, D), 1.0, 6.0, ((0, 64), (2, 8)))
    cache_kv = bell_draw(key_of[10], (INST * SEQ_GRP, 2, CTX, KVH * HD), 1.0, 6.0, ((0, 64), (3, 8)))
    context_lengths = draw_context_lengths(jax.random.fold_in(key_of[12], 71), 0)
    return dict(prompt_states=prompt_states, prompt_lengths=prompt_lengths, prompt_target=prompt_target, prompt_query=prompt_query, prompt_next=prompt_next, key_weight=key_weight, value_weight=value_weight, key_gain=key_gain, seq_query=seq_query, seq_next=seq_next, cache_kv=cache_kv, context_lengths=context_lengths)


EPS = 1e-06
MASKED_SCORE = -1e+30

def head_norm(raw_rows, key_gain):
    return raw_rows * lax.rsqrt(lax.optimization_barrier(jnp.mean(raw_rows * raw_rows, axis=-1, keepdims=True)) + EPS) * key_gain

def finish(raw_key, raw_value, key_gain):
    row_count = raw_key.shape[0]
    head_count = raw_key.shape[1] // HD
    normed_keys = head_norm(raw_key.reshape(row_count, head_count, HD), key_gain).astype(jnp.bfloat16)
    values = raw_value.reshape(row_count, head_count, HD).astype(jnp.bfloat16)
    return lax.optimization_barrier((normed_keys, values))

def rank_within(targets):
    slot_total = targets.shape[1]
    same_target = targets[:, :, None] == targets[:, None, :]
    earlier = jnp.arange(slot_total)[None, :] < jnp.arange(slot_total)[:, None]
    return lax.optimization_barrier(jnp.sum(same_target & earlier[None], axis=2)).astype(jnp.int32)

def attend(queries, old_keys, old_values, old_valid, new_keys, new_values):
    batch_size, step_count = (queries.shape[0], queries.shape[1])
    head_count = old_keys.shape[2]
    grouped = queries.reshape(batch_size, step_count, head_count, QPK, HD).astype(jnp.float32)
    scaling = HD ** (-0.5)
    old_scores = jnp.einsum('bskgd,bckd->bskgc', grouped, old_keys.astype(jnp.float32)) * scaling
    new_scores = jnp.einsum('bskgd,btkd->bskgt', grouped, new_keys.astype(jnp.float32)) * scaling
    old_scores = jnp.where(old_valid[:, None, None, None, :], old_scores, MASKED_SCORE)
    causal = jnp.arange(step_count)[None, :] <= jnp.arange(step_count)[:, None]
    new_scores = jnp.where(causal[None, :, None, None, :], new_scores, MASKED_SCORE)
    highest = jnp.maximum(lax.optimization_barrier(jnp.max(old_scores, axis=-1, keepdims=True)), lax.optimization_barrier(jnp.max(new_scores, axis=-1, keepdims=True)))
    old_exp = jnp.exp(old_scores - highest)
    new_exp = jnp.exp(new_scores - highest)
    totals = lax.optimization_barrier(jnp.sum(old_exp, axis=-1, keepdims=True)) + lax.optimization_barrier(jnp.sum(new_exp, axis=-1, keepdims=True))
    old_prob = lax.optimization_barrier((old_exp / totals).astype(jnp.bfloat16)).astype(jnp.float32)
    new_prob = lax.optimization_barrier((new_exp / totals).astype(jnp.bfloat16)).astype(jnp.float32)
    blended = jnp.einsum('bskgc,bckd->bskgd', old_prob, old_values.astype(jnp.float32))
    blended = blended + jnp.einsum('bskgt,btkd->bskgd', new_prob, new_values.astype(jnp.float32))
    return blended.reshape(batch_size, step_count, head_count * QPK * HD).astype(jnp.bfloat16)

def reference(prompt_states, prompt_lengths, prompt_target, prompt_query, prompt_next, key_weight, value_weight, key_gain, seq_query, seq_next, cache_kv, context_lengths):
    instances = N_POOL * N_GRP

    def project(states):
        raw_key = jnp.dot(states, key_weight, preferred_element_type=jnp.float32)
        raw_value = jnp.dot(states, value_weight, preferred_element_type=jnp.float32)
        return finish(raw_key, raw_value, key_gain)
    prompt_keys, prompt_values = lax.map(project, prompt_states.reshape(instances, TILE, D))
    prompt_keys = prompt_keys.reshape(instances, PSLOT, PLEN, KVH, HD)
    prompt_values = prompt_values.reshape(instances, PSLOT, PLEN, KVH, HD)
    joined_keys, joined_values = project(prompt_next.reshape(instances * PSLOT * STEPS, D))
    joined_keys = joined_keys.reshape(instances, PSLOT, STEPS, KVH, HD)
    joined_values = joined_values.reshape(instances, PSLOT, STEPS, KVH, HD)
    prompt_valid = jnp.arange(PLEN)[None, None, :] < prompt_lengths[:, :, None]

    def joined_block(packed):
        return attend(*packed)
    joined = lax.map(joined_block, (prompt_query.reshape(instances, PSLOT, STEPS, QH * HD), prompt_keys, prompt_values, prompt_valid, joined_keys, joined_values))
    targets = prompt_target[:, :, 0]
    rankings = rank_within(targets)
    sources = jnp.arange(instances).astype(jnp.int32)
    destination = ((sources // N_GRP + 1) % N_POOL)[:, None] * N_GRP + targets
    slot_index = (sources % N_GRP)[:, None] * MOST + rankings
    placed = jnp.zeros((instances, N_GRP * MOST, STEPS, QH * HD), jnp.bfloat16)
    placed = placed.at[destination.reshape(-1), slot_index.reshape(-1)].set(joined.reshape(instances * PSLOT, STEPS, QH * HD))
    seq_keys, seq_values = project(seq_next.reshape(instances * SEQ_GRP * STEPS, D))
    seq_keys = seq_keys.reshape(instances, SEQ_GRP, STEPS, KVH, HD)
    seq_values = seq_values.reshape(instances, SEQ_GRP, STEPS, KVH, HD)
    cache_view = cache_kv.reshape(instances, SEQ_GRP, 2, CTX, KVH, HD)
    context_valid = jnp.arange(CTX)[None, None, :] < context_lengths.reshape(instances, SEQ_GRP)[:, :, None]

    def cached_block(packed):
        queries, cached, valid_rows, step_keys, step_values = packed
        return attend(queries, cached[:, 0], cached[:, 1], valid_rows, step_keys, step_values)
    seq_output = lax.map(cached_block, (seq_query.reshape(instances, SEQ_GRP, STEPS, QH * HD), cache_view, context_valid, seq_keys, seq_values))
    return (seq_output.reshape(instances * SEQ_GRP, STEPS, QH * HD), placed)
```

```python
import functools

import jax
import jax.numpy as jnp
from jax import lax
from jax.experimental import pallas as pl
from jax.experimental.pallas import tpu as pltpu
from jax.sharding import PartitionSpec as P

HD = 128
QPK = 8
MOST = 2
EPS = 1e-06
MASKED_SCORE = -1e30
GROUP = 8
ORDER = (0, 2, 1, 3)
CHUNKS = 1


def exchange(block, axis, apart):
    size = lax.axis_size(axis)
    return lax.ppermute(block, axis, [(i, i ^ apart) for i in range(size)])


def finish(own, received, gain):
    raw = own + received.astype(jnp.float32)
    raw_key = raw[:, :HD]
    scale = lax.rsqrt(jnp.mean(raw_key * raw_key, axis=-1, keepdims=True) + EPS)
    return (raw_key * scale * gain).astype(jnp.bfloat16), raw[:, HD:].astype(jnp.bfloat16)


def contract_last(left, right):
    return lax.dot_general(left, right, (((1,), (1,)), ((), ())), preferred_element_type=jnp.float32)


def attend(query_rows, old_keys, old_values, new_keys, new_values, old_seen, new_seen, out):
    rows = query_rows.shape[0]
    queries = jnp.concatenate([query_rows[:, h * HD : (h + 1) * HD] for h in range(QPK)], axis=0)
    scaling = HD ** (-0.5)
    old_scores = jnp.where(old_seen, contract_last(queries, old_keys) * scaling, MASKED_SCORE)
    new_scores = jnp.where(new_seen, contract_last(queries, new_keys) * scaling, MASKED_SCORE)
    highest = jnp.maximum(
        jnp.max(old_scores, axis=-1, keepdims=True), jnp.max(new_scores, axis=-1, keepdims=True)
    )
    old_exp = jnp.exp(old_scores - highest)
    new_exp = jnp.exp(new_scores - highest)
    totals = jnp.sum(old_exp, axis=-1, keepdims=True) + jnp.sum(new_exp, axis=-1, keepdims=True)
    old_prob = (old_exp / totals).astype(jnp.bfloat16)
    new_prob = (new_exp / totals).astype(jnp.bfloat16)
    blended = jnp.dot(old_prob, old_values, preferred_element_type=jnp.float32) + jnp.dot(
        new_prob, new_values, preferred_element_type=jnp.float32
    )
    blended = blended.astype(jnp.bfloat16)
    for h in range(QPK):
        out[:, h * HD : (h + 1) * HD] = blended[h * rows : (h + 1) * rows, :]


def seen_masks(rows, steps, old_len, old_count, new_count, old_live):
    old_shape, new_shape = (rows * QPK, old_count), (rows * QPK, new_count)
    old_row = lax.broadcasted_iota(jnp.int32, old_shape, 0) & (rows - 1)
    old_col = lax.broadcasted_iota(jnp.int32, old_shape, 1)
    step_bits = steps.bit_length() - 1
    len_bits = old_len.bit_length() - 1
    old_seen = ((old_row >> step_bits) == (old_col >> len_bits)) & (old_live > 0)
    new_row = lax.broadcasted_iota(jnp.int32, new_shape, 0) & (rows - 1)
    new_col = lax.broadcasted_iota(jnp.int32, new_shape, 1)
    new_seen = ((new_row >> step_bits) == (new_col >> step_bits)) & (new_col <= new_row)
    return old_seen, new_seen


def prompt_kernel(
    steps, prompt_len, own_old, got_old, own_new, got_new, gain, live, query, out
):
    old_keys, old_values = finish(own_old[...], got_old[...], gain[...])
    new_keys, new_values = finish(own_new[...], got_new[...], gain[...])
    rows = query.shape[0]
    old_seen, new_seen = seen_masks(
        rows, steps, prompt_len, old_keys.shape[0], new_keys.shape[0], live[0]
    )
    attend(query[...], old_keys, old_values, new_keys, new_values, old_seen, new_seen, out)


def prompt_attention(own_old, got_old, own_new, got_new, gain, live, query, steps, prompt_len):
    new_rows, old_rows = GROUP * steps, GROUP * prompt_len
    groups = query.shape[0] // new_rows
    row_block = lambda count, width: pl.BlockSpec((count, width), lambda g: (g, 0))
    return pl.pallas_call(
        functools.partial(prompt_kernel, steps, prompt_len),
        grid=(groups,),
        in_specs=[
            row_block(old_rows, 2 * HD),
            row_block(old_rows, 2 * HD),
            row_block(new_rows, 2 * HD),
            row_block(new_rows, 2 * HD),
            pl.BlockSpec((1, HD), lambda g: (0, 0)),
            pl.BlockSpec((1, 1, old_rows), lambda g: (g, 0, 0)),
            row_block(new_rows, QPK * HD),
        ],
        out_specs=row_block(new_rows, QPK * HD),
        out_shape=jax.ShapeDtypeStruct(query.shape, jnp.bfloat16),
        compiler_params=pltpu.CompilerParams(vmem_limit_bytes=24 * 2**20),
        cost_estimate=pl.CostEstimate(flops=10**9, bytes_accessed=2 * 10**6, transcendentals=10**5),
        name="prompt_attention",
    )(own_old, got_old, own_new, got_new, gain, live, query)


def cached_kernel(steps, own_new, got_new, gain, live, query, cache, out):
    new_keys, new_values = finish(own_new[...], got_new[...], gain[...])
    sequences, _, context, _ = cache.shape
    old_keys = cache[:, 0].reshape(sequences * context, HD)
    old_values = cache[:, 1].reshape(sequences * context, HD)
    old_seen, new_seen = seen_masks(
        query.shape[0], steps, context, sequences * context, new_keys.shape[0], live[...]
    )
    attend(query[...], old_keys, old_values, new_keys, new_values, old_seen, new_seen, out)


def cached_attention(own_new, got_new, gain, live, query, cache, steps):
    whole = pl.BlockSpec(memory_space=pltpu.VMEM)
    return pl.pallas_call(
        functools.partial(cached_kernel, steps),
        in_specs=[whole] * 6,
        out_specs=whole,
        out_shape=jax.ShapeDtypeStruct(query.shape, jnp.bfloat16),
        compiler_params=pltpu.CompilerParams(vmem_limit_bytes=24 * 2**20),
        cost_estimate=pl.CostEstimate(flops=10**9, bytes_accessed=2 * 10**6, transcendentals=10**5),
        name="cached_attention",
    )(own_new, got_new, gain, live, query, cache)


def rank_within(targets):
    slot_total = targets.shape[0]
    same_target = targets[:, None] == targets[None, :]
    earlier = jnp.arange(slot_total)[None, :] < jnp.arange(slot_total)[:, None]
    return jnp.sum(same_target & earlier, axis=1)


def on_device(
    prompt_states,
    prompt_lengths,
    prompt_target,
    prompt_query,
    prompt_next,
    key_weight,
    value_weight,
    key_gain,
    seq_query,
    seq_next,
    cache_kv,
    context_lengths,
):
    groups = lax.axis_size("grp")
    pool_index = lax.axis_index("pool")
    group_index = lax.axis_index("grp")
    lane = lax.axis_index("tp")
    prompts = prompt_query.shape[0]
    prompt_len = prompt_states.shape[0] // prompts
    seq_count, steps, query_width = seq_query.shape
    width = prompt_next.shape[2]
    quad = len(ORDER)

    share = quad * width // groups
    per_block = groups // quad
    block_number = jnp.asarray(ORDER, jnp.int32)[group_index // per_block]
    start = ((lane ^ 4) ^ block_number) * width + (group_index % per_block) * share
    weight_share = jnp.concatenate(
        [
            lax.dynamic_slice_in_dim(key_weight, start, share, 0),
            lax.dynamic_slice_in_dim(value_weight, start, share, 0),
        ],
        axis=1,
    )
    partner_weight = lax.all_gather(exchange(weight_share, "tp", 4), "grp", axis=0, tiled=True)
    own_weight = jnp.concatenate(
        [
            jnp.concatenate(
                [
                    lax.dynamic_slice_in_dim(weight, (lane ^ k) * width, width, 0)
                    for weight in (key_weight, value_weight)
                ],
                axis=1,
            )
            for k in ORDER
        ],
        axis=0,
    )

    gain = key_gain.reshape(1, HD)
    instance = pool_index * groups + group_index
    lengths = lax.dynamic_index_in_dim(prompt_lengths, instance, 0, keepdims=False)
    prompt_live = (jnp.arange(prompt_len)[None, :] < lengths[:, None]).astype(jnp.int32)
    prompt_live = prompt_live.reshape(prompts // GROUP, 1, GROUP * prompt_len)
    context = cache_kv.shape[2]
    seq_live = (jnp.arange(context)[None, :] < context_lengths[:, None]).astype(jnp.int32)
    seq_live = seq_live.reshape(1, seq_count * context)

    query_rows = prompt_query.reshape(prompts * steps, query_width)
    next_rows = prompt_next.reshape(prompts * steps, width)
    seq_rows = seq_next.reshape(seq_count * steps, width)

    part = prompts // CHUNKS
    old_rows, new_rows = part * prompt_len, part * steps
    outputs = []
    seq_output = None
    for c in range(CHUNKS):
        blocks = [
            prompt_states[c * old_rows : (c + 1) * old_rows],
            next_rows[c * new_rows : (c + 1) * new_rows],
        ]
        if c == CHUNKS - 1:
            blocks.append(seq_rows)
        mine = jnp.concatenate(blocks, axis=0)
        second = exchange(mine, "tp", 2)
        first = exchange(mine, "tp", 1)
        third = exchange(second, "tp", 1)
        features = (mine, second, first, third)

        def partial_sum(weight):
            return sum(
                jnp.dot(
                    block,
                    weight[k * width : (k + 1) * width],
                    preferred_element_type=jnp.float32,
                )
                for k, block in enumerate(features)
            )

        sent = partial_sum(partner_weight).astype(jnp.bfloat16)
        got = exchange(sent, "tp", 4)
        own = partial_sum(own_weight)
        outputs.append(
            prompt_attention(
                own[:old_rows],
                got[:old_rows],
                own[old_rows : old_rows + new_rows],
                got[old_rows : old_rows + new_rows],
                gain,
                prompt_live[c * part // GROUP : (c + 1) * part // GROUP],
                query_rows[c * new_rows : (c + 1) * new_rows],
                steps,
                prompt_len,
            )
        )
        if c == CHUNKS - 1:
            seq_output = cached_attention(
                own[old_rows + new_rows :],
                got[old_rows + new_rows :],
                gain,
                seq_live,
                seq_query.reshape(seq_count * steps, query_width),
                cache_kv,
                steps,
            ).reshape(seq_count, steps, query_width)

    crossed = [exchange(block, "pool", 1) for block in outputs]
    source = (pool_index ^ 1) * groups + group_index
    targets = lax.dynamic_index_in_dim(prompt_target[:, :, 0], source, 0, keepdims=False)
    places = targets * MOST + rank_within(targets)
    place_rows = (places[:, None] * steps + jnp.arange(steps)[None, :]).reshape(-1)
    chooser = (jnp.arange(groups * MOST * steps)[:, None] == place_rows[None, :]).astype(
        jnp.bfloat16
    )
    outgoing = sum(
        jnp.dot(
            chooser[:, c * new_rows : (c + 1) * new_rows],
            crossed[c],
            preferred_element_type=jnp.float32,
        )
        for c in range(CHUNKS)
    ).astype(jnp.bfloat16)
    arrived = lax.all_to_all(outgoing, "grp", split_axis=0, concat_axis=0, tiled=True)
    return seq_output, arrived.reshape(1, groups * MOST, steps, query_width)


def solution(mesh):
    return jax.shard_map(
        on_device,
        mesh=mesh,
        in_specs=(
            P(("pool", "grp"), "tp"),
            P(),
            P(),
            P(("pool", "grp"), None, "tp"),
            P(("pool", "grp"), None, "tp"),
            P(None, "tp"),
            P(None, "tp"),
            P(),
            P(("pool", "grp"), None, "tp"),
            P(("pool", "grp"), None, "tp"),
            P(("pool", "grp"), None, None, "tp"),
            P(("pool", "grp")),
        ),
        out_specs=(P(("pool", "grp"), None, "tp"), P(("pool", "grp"), None, None, "tp")),
        check_vma=False,
    )
```

```python
import functools

import jax
import jax.numpy as jnp
from jax import lax
from jax.experimental import pallas as pl
from jax.experimental.pallas import tpu as pltpu
from jax.sharding import PartitionSpec as P

HD = 128
QPK = 8
MOST = 2
EPS = 1e-06
MASKED_SCORE = -1e30
GROUP = 8
QUAD = 4
BUCKETS = (384,)


def exchange(block, axis, apart):
    size = lax.axis_size(axis)
    return lax.ppermute(block, axis, [(i, i ^ apart) for i in range(size)])


def finish(own, received, gain):
    raw = own + received.astype(jnp.float32)
    raw_key = raw[:, :HD]
    scale = lax.rsqrt(jnp.mean(raw_key * raw_key, axis=-1, keepdims=True) + EPS)
    return (raw_key * scale * gain).astype(jnp.bfloat16), raw[:, HD:].astype(jnp.bfloat16)


def contract_last(left, right):
    return lax.dot_general(left, right, (((1,), (1,)), ((), ())), preferred_element_type=jnp.float32)


def attend(query_rows, old_keys, old_values, new_keys, new_values, old_seen, new_seen, out):
    rows = query_rows.shape[0]
    queries = jnp.concatenate([query_rows[:, h * HD : (h + 1) * HD] for h in range(QPK)], axis=0)
    scaling = HD ** (-0.5)
    old_scores = jnp.where(old_seen, contract_last(queries, old_keys) * scaling, MASKED_SCORE)
    new_scores = jnp.where(new_seen, contract_last(queries, new_keys) * scaling, MASKED_SCORE)
    highest = jnp.maximum(
        jnp.max(old_scores, axis=-1, keepdims=True), jnp.max(new_scores, axis=-1, keepdims=True)
    )
    old_exp = jnp.exp(old_scores - highest)
    new_exp = jnp.exp(new_scores - highest)
    totals = jnp.sum(old_exp, axis=-1, keepdims=True) + jnp.sum(new_exp, axis=-1, keepdims=True)
    old_prob = (old_exp / totals).astype(jnp.bfloat16)
    new_prob = (new_exp / totals).astype(jnp.bfloat16)
    blended = jnp.dot(old_prob, old_values, preferred_element_type=jnp.float32) + jnp.dot(
        new_prob, new_values, preferred_element_type=jnp.float32
    )
    blended = blended.astype(jnp.bfloat16)
    for h in range(QPK):
        out[:, h * HD : (h + 1) * HD] = blended[h * rows : (h + 1) * rows, :]


def new_mask(rows, steps, count, first):
    shape = (rows * QPK, count)
    step_bits = steps.bit_length() - 1
    row = (lax.broadcasted_iota(jnp.int32, shape, 0) & (rows - 1)) + first
    column = lax.broadcasted_iota(jnp.int32, shape, 1)
    return ((row >> step_bits) == (column >> step_bits)) & (column <= row)


def old_mask(rows, steps, owners, first):
    shape = (rows * QPK, owners.shape[1])
    step_bits = steps.bit_length() - 1
    row = (lax.broadcasted_iota(jnp.int32, shape, 0) & (rows - 1)) + first
    return (row >> step_bits) == owners


def pack_kernel(place, states, nexts, sequences, packed):
    kept = packed.shape[0] - nexts.shape[0] - sequences.shape[0]
    row = lax.broadcasted_iota(jnp.int32, (kept, place.shape[1]), 0)
    chooser = (row == place[...]).astype(jnp.float32).astype(jnp.bfloat16)
    live = jnp.dot(chooser, states[...], preferred_element_type=jnp.float32)
    packed[:kept, :] = live.astype(jnp.bfloat16)
    packed[kept : kept + nexts.shape[0], :] = nexts[...]
    packed[kept + nexts.shape[0] :, :] = sequences[...]


def pack(place, states, nexts, sequences, kept):
    whole = pl.BlockSpec(memory_space=pltpu.VMEM)
    rows = kept + nexts.shape[0] + sequences.shape[0]
    return pl.pallas_call(
        pack_kernel,
        in_specs=[whole] * 4,
        out_specs=whole,
        out_shape=jax.ShapeDtypeStruct((rows, states.shape[1]), jnp.bfloat16),
        compiler_params=pltpu.CompilerParams(vmem_limit_bytes=24 * 2**20),
        name="pack",
    )(place, states, nexts, sequences)


def prompt_kernel(steps, own, got, gain, owners, query, out):
    kept = owners.shape[1]
    count = query.shape[0]
    old_keys, old_values = finish(own[:kept], got[:kept], gain[...])
    new_keys, new_values = finish(own[kept : kept + count], got[kept : kept + count], gain[...])
    rows = GROUP * steps
    for first in range(0, count, rows):
        attend(
            query[first : first + rows],
            old_keys,
            old_values,
            new_keys[first : first + rows],
            new_values[first : first + rows],
            old_mask(rows, steps, owners[...], first),
            new_mask(rows, steps, rows, 0),
            out.at[pl.ds(first, rows)],
        )


def prompt_attention(own, got, gain, owners, query, steps):
    whole = pl.BlockSpec(memory_space=pltpu.VMEM)
    return pl.pallas_call(
        functools.partial(prompt_kernel, steps),
        in_specs=[whole] * 5,
        out_specs=whole,
        out_shape=jax.ShapeDtypeStruct(query.shape, jnp.bfloat16),
        compiler_params=pltpu.CompilerParams(vmem_limit_bytes=32 * 2**20),
        cost_estimate=pl.CostEstimate(flops=10**9, bytes_accessed=2 * 10**6, transcendentals=10**5),
        name="prompt_attention",
    )(own, got, gain, owners, query)


def cached_kernel(steps, own_new, got_new, gain, owners, query, cache, out):
    new_keys, new_values = finish(own_new[...], got_new[...], gain[...])
    sequences, _, context, _ = cache.shape
    old_keys = cache[:, 0].reshape(sequences * context, HD)
    old_values = cache[:, 1].reshape(sequences * context, HD)
    rows = query.shape[0]
    attend(
        query[...],
        old_keys,
        old_values,
        new_keys,
        new_values,
        old_mask(rows, steps, owners[...], 0),
        new_mask(rows, steps, rows, 0),
        out,
    )


def cached_attention(own, got, gain, owners, query, cache, steps):
    rows = query.shape[0]
    last = own.shape[0] // rows - 1
    fresh = pl.BlockSpec((rows, 2 * HD), lambda g: (last, 0))
    return pl.pallas_call(
        functools.partial(cached_kernel, steps),
        grid=(1,),
        in_specs=[
            fresh,
            fresh,
            pl.BlockSpec((1, HD), lambda g: (0, 0)),
            pl.BlockSpec(owners.shape, lambda g: (0, 0)),
            pl.BlockSpec(query.shape, lambda g: (0, 0)),
            pl.BlockSpec(cache.shape, lambda g: (0, 0, 0, 0)),
        ],
        out_specs=pl.BlockSpec(query.shape, lambda g: (0, 0)),
        out_shape=jax.ShapeDtypeStruct(query.shape, jnp.bfloat16),
        compiler_params=pltpu.CompilerParams(vmem_limit_bytes=24 * 2**20),
        cost_estimate=pl.CostEstimate(flops=10**9, bytes_accessed=2 * 10**6, transcendentals=10**5),
        name="cached_attention",
    )(own, got, gain, owners, query, cache)


def spread(share):
    copies = jnp.broadcast_to(share[None], (lax.axis_size("grp"),) + share.shape)
    arrived = lax.all_to_all(copies, "grp", split_axis=0, concat_axis=0, tiled=True)
    return arrived.reshape(-1, share.shape[1])


def project_kernel(order, block_number, *refs):
    features, (key_block, value_block, partner_block, own, sent, total) = refs[:-6], refs[-6:]
    k = pl.program_id(0)

    @pl.when(k == 0)
    def _():
        total[...] = jnp.zeros_like(total)

    def add(block):
        weight = jnp.concatenate([key_block[...], value_block[...], partner_block[...]], axis=1)
        total[...] += jnp.dot(block[...], weight, preferred_element_type=jnp.float32)

    for index, block in enumerate(features):
        pl.when(k == index)(functools.partial(add, block))

    @pl.when(k == pl.num_programs(0) - 1)
    def _():
        own[...] = total[:, : 2 * HD]
        sent[...] = total[:, 2 * HD :].astype(jnp.bfloat16)


def project(features, order, block_number, weights):
    rows, width = features[0].shape
    own_spec = pl.BlockSpec((width, HD), lambda k, o, b: (b[k], 0))
    whole = pl.BlockSpec((rows, 2 * HD), lambda k, o, b: (0, 0))
    return pl.pallas_call(
        project_kernel,
        grid_spec=pltpu.PrefetchScalarGridSpec(
            num_scalar_prefetch=2,
            grid=(QUAD,),
            in_specs=[pl.BlockSpec((rows, width), lambda k, o, b: (0, 0))] * QUAD
            + [own_spec, own_spec, pl.BlockSpec((width, 2 * HD), lambda k, o, b: (o[k], 0))],
            out_specs=[whole, whole],
            scratch_shapes=[pltpu.VMEM((rows, 4 * HD), jnp.float32)],
        ),
        out_shape=[
            jax.ShapeDtypeStruct((rows, 2 * HD), jnp.float32),
            jax.ShapeDtypeStruct((rows, 2 * HD), jnp.bfloat16),
        ],
        compiler_params=pltpu.CompilerParams(vmem_limit_bytes=32 * 2**20),
        cost_estimate=pl.CostEstimate(
            flops=2 * rows * width * QUAD * 4 * HD, bytes_accessed=8 * 10**6, transcendentals=0
        ),
        name="project",
    )(order, block_number, *features, *weights)


def pass_on(block, awaited):
    anywhere = pl.BlockSpec(memory_space=pl.ANY)
    return pl.pallas_call(
        lambda block_ref, awaited_ref, out_ref: None,
        in_specs=[anywhere, anywhere],
        out_specs=anywhere,
        out_shape=jax.ShapeDtypeStruct(block.shape, block.dtype),
        input_output_aliases={0: 0},
        name="pass_on",
    )(block, awaited)


def rank_within(targets):
    slot_total = targets.shape[0]
    same_target = targets[:, None] == targets[None, :]
    earlier = jnp.arange(slot_total)[None, :] < jnp.arange(slot_total)[:, None]
    return jnp.sum(same_target & earlier, axis=1)


def run(
    kept,
    prompt_states,
    prompt_lengths,
    prompt_target,
    prompt_query,
    prompt_next,
    key_weight,
    value_weight,
    key_gain,
    seq_query,
    seq_next,
    cache_kv,
    context_lengths,
):
    groups = lax.axis_size("grp")
    pool_index = lax.axis_index("pool")
    group_index = lax.axis_index("grp")
    lane = lax.axis_index("tp")
    prompts = prompt_query.shape[0]
    prompt_len = prompt_states.shape[0] // prompts
    seq_count, steps, query_width = seq_query.shape
    width = prompt_next.shape[2]
    quad = QUAD

    share = quad * width // groups
    start = ((lane ^ 4) // quad * quad) * width + group_index * share
    weight_share = jnp.concatenate(
        [
            lax.dynamic_slice_in_dim(key_weight, start, share, 0),
            lax.dynamic_slice_in_dim(value_weight, start, share, 0),
        ],
        axis=1,
    )
    received_share = exchange(weight_share, "tp", 4)
    partner_weight = spread(received_share)
    gain = key_gain.reshape(1, HD)
    instance = pool_index * groups + group_index
    lengths = lax.dynamic_index_in_dim(prompt_lengths, instance, 0, keepdims=False)
    ends = jnp.cumsum(lengths)
    position = jnp.arange(prompt_len)[None, :]
    place = jnp.where(position < lengths[:, None], (ends - lengths)[:, None] + position, -1)
    place = place.reshape(1, prompts * prompt_len).astype(jnp.int32)
    prompt_owners = jnp.sum(ends[:, None] <= jnp.arange(kept)[None, :], axis=0, dtype=jnp.int32)
    prompt_owners = prompt_owners.reshape(1, kept)
    context = cache_kv.shape[2]
    seq_owners = jnp.where(
        jnp.arange(context)[None, :] < context_lengths[:, None],
        jnp.arange(seq_count, dtype=jnp.int32)[:, None],
        seq_count,
    ).reshape(1, seq_count * context)

    query_rows = prompt_query.reshape(prompts * steps, query_width)
    mine = pack(
        place,
        prompt_states,
        prompt_next.reshape(prompts * steps, width),
        seq_next.reshape(seq_count * steps, width),
        kept,
    )
    mine = pass_on(mine, received_share)
    second = exchange(mine, "tp", 2)
    first = exchange(mine, "tp", 1)
    second = pass_on(second, first)
    third = exchange(second, "tp", 1)
    order = jnp.asarray([0, 1, 2, 3], jnp.int32) ^ (lane % quad)
    own, sent = project(
        [mine, first, second, third],
        order,
        lane // quad * quad + order,
        (key_weight, value_weight, partner_weight),
    )
    got = exchange(sent, "tp", 4)
    result = prompt_attention(own, got, gain, prompt_owners, query_rows, steps)
    crossed = exchange(result, "pool", 1)
    seq_output = cached_attention(
        own,
        got,
        gain,
        seq_owners,
        seq_query.reshape(seq_count * steps, query_width),
        cache_kv,
        steps,
    ).reshape(seq_count, steps, query_width)

    source = (pool_index ^ 1) * groups + group_index
    targets = lax.dynamic_index_in_dim(prompt_target[:, :, 0], source, 0, keepdims=False)
    places = targets * MOST + rank_within(targets)
    place_rows = (places[:, None] * steps + jnp.arange(steps)[None, :]).reshape(-1)
    chooser = (jnp.arange(groups * MOST * steps)[:, None] == place_rows[None, :]).astype(
        jnp.bfloat16
    )
    outgoing = jnp.dot(chooser, crossed, preferred_element_type=jnp.float32).astype(jnp.bfloat16)
    arrived = lax.all_to_all(outgoing, "grp", split_axis=0, concat_axis=0, tiled=True)
    return seq_output, arrived.reshape(1, groups * MOST, steps, query_width)


def on_device(*arrays):
    rows = arrays[0].shape[0]
    most = jnp.max(jnp.sum(arrays[1], axis=1))
    sizes = [size for size in BUCKETS if size < rows] + [rows]
    choice = sum((most > size).astype(jnp.int32) for size in sizes[:-1])
    return lax.switch(choice, [functools.partial(run, size) for size in sizes], *arrays)


def solution(mesh):
    return jax.shard_map(
        on_device,
        mesh=mesh,
        in_specs=(
            P(("pool", "grp"), "tp"),
            P(),
            P(),
            P(("pool", "grp"), None, "tp"),
            P(("pool", "grp"), None, "tp"),
            P(None, "tp"),
            P(None, "tp"),
            P(),
            P(("pool", "grp"), None, "tp"),
            P(("pool", "grp"), None, "tp"),
            P(("pool", "grp"), None, None, "tp"),
            P(("pool", "grp")),
        ),
        out_specs=(P(("pool", "grp"), None, "tp"), P(("pool", "grp"), None, None, "tp")),
        check_vma=False,
    )
```

```python
import functools

import jax
import jax.numpy as jnp
from jax import lax
from jax.experimental import pallas as pl
from jax.experimental.pallas import tpu as pltpu
from jax.sharding import PartitionSpec as P

HD = 128
QPK = 8
MOST = 2
EPS = 1e-06
MASKED_SCORE = -1e30
GROUP = 8
QUAD = 4
BUCKETS = (336, 352, 368, 384)


def exchange(block, axis, apart):
    size = lax.axis_size(axis)
    return lax.ppermute(block, axis, [(i, i ^ apart) for i in range(size)])


def finish(own, received, gain):
    raw = own + received.astype(jnp.float32)
    raw_key = raw[:, :HD]
    scale = lax.rsqrt(jnp.mean(raw_key * raw_key, axis=-1, keepdims=True) + EPS)
    return (raw_key * scale * gain).astype(jnp.bfloat16), raw[:, HD:].astype(jnp.bfloat16)


def contract_last(left, right):
    return lax.dot_general(left, right, (((1,), (1,)), ((), ())), preferred_element_type=jnp.float32)


def attend(query_rows, old_keys, old_values, new_keys, new_values, old_seen, new_seen, out):
    rows = query_rows.shape[0]
    queries = jnp.concatenate([query_rows[:, h * HD : (h + 1) * HD] for h in range(QPK)], axis=0)
    scaling = HD ** (-0.5)
    old_scores = jnp.where(old_seen, contract_last(queries, old_keys) * scaling, MASKED_SCORE)
    new_scores = jnp.where(new_seen, contract_last(queries, new_keys) * scaling, MASKED_SCORE)
    highest = jnp.maximum(
        jnp.max(old_scores, axis=-1, keepdims=True), jnp.max(new_scores, axis=-1, keepdims=True)
    )
    old_exp = jnp.exp(old_scores - highest)
    new_exp = jnp.exp(new_scores - highest)
    totals = jnp.sum(old_exp, axis=-1, keepdims=True) + jnp.sum(new_exp, axis=-1, keepdims=True)
    old_prob = (old_exp / totals).astype(jnp.bfloat16)
    new_prob = (new_exp / totals).astype(jnp.bfloat16)
    blended = jnp.dot(old_prob, old_values, preferred_element_type=jnp.float32) + jnp.dot(
        new_prob, new_values, preferred_element_type=jnp.float32
    )
    blended = blended.astype(jnp.bfloat16)
    for h in range(QPK):
        out[:, h * HD : (h + 1) * HD] = blended[h * rows : (h + 1) * rows, :]


def new_mask(rows, steps, count, first):
    shape = (rows * QPK, count)
    step_bits = steps.bit_length() - 1
    row = (lax.broadcasted_iota(jnp.int32, shape, 0) & (rows - 1)) + first
    column = lax.broadcasted_iota(jnp.int32, shape, 1)
    return ((row >> step_bits) == (column >> step_bits)) & (column <= row)


def old_mask(rows, steps, owners, first):
    shape = (rows * QPK, owners.shape[1])
    step_bits = steps.bit_length() - 1
    row = (lax.broadcasted_iota(jnp.int32, shape, 0) & (rows - 1)) + first
    return (row >> step_bits) == owners


def pack_kernel(place, states, nexts, sequences, packed):
    next_rows = nexts[...].reshape(-1, packed.shape[1])
    sequence_rows = sequences[...].reshape(-1, packed.shape[1])
    kept = packed.shape[0] - next_rows.shape[0] - sequence_rows.shape[0]
    row = lax.broadcasted_iota(jnp.int32, (kept, place.shape[1]), 0)
    chooser = (row == place[...]).astype(jnp.float32).astype(jnp.bfloat16)
    live = jnp.dot(chooser, states[...], preferred_element_type=jnp.float32)
    packed[:kept, :] = live.astype(jnp.bfloat16)
    packed[kept : kept + next_rows.shape[0], :] = next_rows
    packed[kept + next_rows.shape[0] :, :] = sequence_rows


def pack(place, states, nexts, sequences, kept):
    whole = pl.BlockSpec(memory_space=pltpu.VMEM)
    rows = kept + nexts.shape[0] * nexts.shape[1] + sequences.shape[0] * sequences.shape[1]
    return pl.pallas_call(
        pack_kernel,
        in_specs=[whole] * 4,
        out_specs=whole,
        out_shape=jax.ShapeDtypeStruct((rows, states.shape[1]), jnp.bfloat16),
        compiler_params=pltpu.CompilerParams(vmem_limit_bytes=24 * 2**20),
        name="pack",
    )(place, states, nexts, sequences)


def prompt_kernel(steps, own, got, gain, owners, query, out):
    kept = owners.shape[1]
    count = query.shape[0]
    keys, values = finish(own[: kept + count], got[: kept + count], gain[...])
    old_keys, old_values = keys[:kept], values[:kept]
    new_keys, new_values = keys[kept:], values[kept:]
    rows = GROUP * steps
    for first in range(0, count, rows):
        attend(
            query[first : first + rows],
            old_keys,
            old_values,
            new_keys[first : first + rows],
            new_values[first : first + rows],
            old_mask(rows, steps, owners[...], first),
            new_mask(rows, steps, rows, 0),
            out.at[pl.ds(first, rows)],
        )


def prompt_attention(own, got, gain, owners, query, steps):
    whole = pl.BlockSpec(memory_space=pltpu.VMEM)
    return pl.pallas_call(
        functools.partial(prompt_kernel, steps),
        in_specs=[whole] * 5,
        out_specs=whole,
        out_shape=jax.ShapeDtypeStruct(query.shape, jnp.bfloat16),
        compiler_params=pltpu.CompilerParams(vmem_limit_bytes=32 * 2**20),
        cost_estimate=pl.CostEstimate(flops=10**9, bytes_accessed=2 * 10**6, transcendentals=10**5),
        name="prompt_attention",
    )(own, got, gain, owners, query)


def cached_kernel(steps, own_new, got_new, gain, owners, query, cache, out):
    new_keys, new_values = finish(own_new[...], got_new[...], gain[...])
    sequences, _, context, _ = cache.shape
    old_keys = cache[:, 0].reshape(sequences * context, HD)
    old_values = cache[:, 1].reshape(sequences * context, HD)
    rows = query.shape[0]
    attend(
        query[...],
        old_keys,
        old_values,
        new_keys,
        new_values,
        old_mask(rows, steps, owners[...], 0),
        new_mask(rows, steps, rows, 0),
        out,
    )


def cached_attention(own, got, gain, owners, query, cache, steps):
    rows = query.shape[0]
    last = own.shape[0] // rows - 1
    fresh = pl.BlockSpec((rows, 2 * HD), lambda g: (last, 0))
    return pl.pallas_call(
        functools.partial(cached_kernel, steps),
        grid=(1,),
        in_specs=[
            fresh,
            fresh,
            pl.BlockSpec((1, HD), lambda g: (0, 0)),
            pl.BlockSpec(owners.shape, lambda g: (0, 0)),
            pl.BlockSpec(query.shape, lambda g: (0, 0)),
            pl.BlockSpec(cache.shape, lambda g: (0, 0, 0, 0)),
        ],
        out_specs=pl.BlockSpec(query.shape, lambda g: (0, 0)),
        out_shape=jax.ShapeDtypeStruct(query.shape, jnp.bfloat16),
        compiler_params=pltpu.CompilerParams(vmem_limit_bytes=24 * 2**20),
        cost_estimate=pl.CostEstimate(flops=10**9, bytes_accessed=2 * 10**6, transcendentals=10**5),
        name="cached_attention",
    )(own, got, gain, owners, query, cache)


def spread(share):
    copies = jnp.broadcast_to(share[None], (lax.axis_size("grp"),) + share.shape)
    arrived = lax.all_to_all(copies, "grp", split_axis=0, concat_axis=0, tiled=True)
    return arrived.reshape(-1, share.shape[1])


def multiply_kernel(count, order, block_number, *refs):
    features, weights, (begun, result, total) = refs[:count], refs[count:-3], refs[-3:]
    k = pl.program_id(0)

    @pl.when(k == 0)
    def _():
        total[...] = jnp.broadcast_to(begun[...], total.shape)

    def add(block):
        weight = jnp.concatenate([block_ref[...] for block_ref in weights], axis=1)
        total[...] += jnp.dot(block[...], weight, preferred_element_type=jnp.float32)

    for index, block in enumerate(features):
        pl.when(k == index)(functools.partial(add, block))

    @pl.when(k == pl.num_programs(0) - 1)
    def _():
        result[...] = total[...].astype(result.dtype)


def multiply(begun, features, order, block_number, weights, by_block, dtype):
    rows, width = features[0].shape
    columns = begun.shape[1]
    number = lambda o, b, k: b[k] if by_block else o[k]
    whole = lambda *shape: pl.BlockSpec(shape, lambda k, o, b: (0, 0))
    return pl.pallas_call(
        functools.partial(multiply_kernel, len(features)),
        grid_spec=pltpu.PrefetchScalarGridSpec(
            num_scalar_prefetch=2,
            grid=(len(features),),
            in_specs=[whole(rows, width)] * len(features)
            + [
                pl.BlockSpec((width, weight.shape[1]), lambda k, o, b: (number(o, b, k), 0))
                for weight in weights
            ]
            + [whole(rows if begun.shape[0] == rows else 1, columns)],
            out_specs=whole(rows, columns),
            scratch_shapes=[pltpu.VMEM((rows, columns), jnp.float32)],
        ),
        out_shape=jax.ShapeDtypeStruct((rows, columns), dtype),
        compiler_params=pltpu.CompilerParams(vmem_limit_bytes=24 * 2**20),
        cost_estimate=pl.CostEstimate(
            flops=2 * len(features) * rows * width * columns,
            bytes_accessed=2 * 10**6,
            transcendentals=0,
        ),
        name="multiply",
    )(order, block_number, *features, *weights, begun)


def pass_on(block, awaited, flops=0):
    anywhere = pl.BlockSpec(memory_space=pl.ANY)
    return pl.pallas_call(
        lambda block_ref, awaited_ref, out_ref: None,
        in_specs=[anywhere, anywhere],
        out_specs=anywhere,
        out_shape=jax.ShapeDtypeStruct(block.shape, block.dtype),
        input_output_aliases={0: 0},
        cost_estimate=pl.CostEstimate(flops=flops, bytes_accessed=flops // 300, transcendentals=0),
        name="pass_on",
    )(block, awaited)


def rank_within(targets):
    slot_total = targets.shape[0]
    same_target = targets[:, None] == targets[None, :]
    earlier = jnp.arange(slot_total)[None, :] < jnp.arange(slot_total)[:, None]
    return jnp.sum(same_target & earlier, axis=1)


def run(
    kept,
    prompt_states,
    prompt_lengths,
    prompt_target,
    prompt_query,
    prompt_next,
    key_weight,
    value_weight,
    key_gain,
    seq_query,
    seq_next,
    cache_kv,
    context_lengths,
):
    groups = lax.axis_size("grp")
    pool_index = lax.axis_index("pool")
    group_index = lax.axis_index("grp")
    lane = lax.axis_index("tp")
    prompts = prompt_query.shape[0]
    prompt_len = prompt_states.shape[0] // prompts
    seq_count, steps, query_width = seq_query.shape
    width = prompt_next.shape[2]
    quad = QUAD

    share = quad * width // groups
    start = ((lane ^ 4) // quad * quad) * width + group_index * share
    weight_share = jnp.concatenate(
        [
            lax.dynamic_slice_in_dim(key_weight, start, share, 0),
            lax.dynamic_slice_in_dim(value_weight, start, share, 0),
        ],
        axis=1,
    )
    gain = key_gain.reshape(1, HD)
    instance = pool_index * groups + group_index
    lengths = lax.dynamic_index_in_dim(prompt_lengths, instance, 0, keepdims=False)
    ends = jnp.cumsum(lengths)
    position = jnp.arange(prompt_len)[None, :]
    place = jnp.where(position < lengths[:, None], (ends - lengths)[:, None] + position, -1)
    place = place.reshape(1, prompts * prompt_len).astype(jnp.int32)
    prompt_owners = jnp.sum(ends[:, None] <= jnp.arange(kept)[None, :], axis=0, dtype=jnp.int32)
    prompt_owners = prompt_owners.reshape(1, kept)
    context = cache_kv.shape[2]
    seq_owners = jnp.where(
        jnp.arange(context)[None, :] < context_lengths[:, None],
        jnp.arange(seq_count, dtype=jnp.int32)[:, None],
        seq_count,
    ).reshape(1, seq_count * context)

    query_rows = prompt_query.reshape(prompts * steps, query_width)
    mine = pack(
        place,
        prompt_states,
        prompt_next,
        seq_next,
        kept,
    )
    received_share = exchange(pass_on(weight_share, mine), "tp", 4)
    partner_weight = spread(received_share)

    order = jnp.asarray([0, 1, 2, 3], jnp.int32) ^ (lane % quad)
    block_number = lane // quad * quad + order
    mine = pass_on(mine, received_share)
    second = exchange(mine, "tp", 2)
    first = exchange(mine, "tp", 1)
    second = pass_on(second, first, 8000000000)
    third = exchange(second, "tp", 1)
    blank = jnp.zeros((1, 2 * HD), jnp.float32)
    near = (mine, first, second)
    begun = multiply(
        blank, near, order[:3], block_number[:3], [partner_weight], False, jnp.float32
    )
    sent = multiply(
        begun, [third], order[3:], block_number[3:], [partner_weight], False, jnp.bfloat16
    )
    got = exchange(sent, "tp", 4)
    own = multiply(
        blank,
        near + (third,),
        order,
        block_number,
        [key_weight, value_weight],
        True,
        jnp.float32,
    )
    result = prompt_attention(own, got, gain, prompt_owners, query_rows, steps)
    crossed = exchange(result, "pool", 1)
    seq_output = cached_attention(
        own,
        got,
        gain,
        seq_owners,
        seq_query.reshape(seq_count * steps, query_width),
        cache_kv,
        steps,
    ).reshape(seq_count, steps, query_width)

    source = (pool_index ^ 1) * groups + group_index
    targets = lax.dynamic_index_in_dim(prompt_target[:, :, 0], source, 0, keepdims=False)
    places = targets * MOST + rank_within(targets)
    place_rows = (places[:, None] * steps + jnp.arange(steps)[None, :]).reshape(-1)
    chooser = (jnp.arange(groups * MOST * steps)[:, None] == place_rows[None, :]).astype(
        jnp.bfloat16
    )
    outgoing = jnp.dot(chooser, crossed, preferred_element_type=jnp.float32).astype(jnp.bfloat16)
    arrived = lax.all_to_all(outgoing, "grp", split_axis=0, concat_axis=0, tiled=True)
    return seq_output, arrived.reshape(1, groups * MOST, steps, query_width)


def on_device(*arrays):
    rows = arrays[0].shape[0]
    most = jnp.max(jnp.sum(arrays[1], axis=1))
    sizes = [size for size in BUCKETS if size < rows] + [rows]
    choice = sum((most > size).astype(jnp.int32) for size in sizes[:-1])
    return lax.switch(choice, [functools.partial(run, size) for size in sizes], *arrays)


def solution(mesh):
    return jax.shard_map(
        on_device,
        mesh=mesh,
        in_specs=(
            P(("pool", "grp"), "tp"),
            P(),
            P(),
            P(("pool", "grp"), None, "tp"),
            P(("pool", "grp"), None, "tp"),
            P(None, "tp"),
            P(None, "tp"),
            P(),
            P(("pool", "grp"), None, "tp"),
            P(("pool", "grp"), None, "tp"),
            P(("pool", "grp"), None, None, "tp"),
            P(("pool", "grp")),
        ),
        out_specs=(P(("pool", "grp"), None, "tp"), P(("pool", "grp"), None, None, "tp")),
        check_vma=False,
    )
```

```python
import functools

import jax
import jax.numpy as jnp
from jax import lax
from jax.experimental import pallas as pl
from jax.experimental.pallas import tpu as pltpu
from jax.sharding import PartitionSpec as P

HD = 128
QPK = 8
MOST = 2
EPS = 1e-06
MASKED_SCORE = -1e30
GROUP = 8
QUAD = 4
BUCKETS = (336, 352, 368, 384)


def exchange(block, axis, apart):
    size = lax.axis_size(axis)
    return lax.ppermute(block, axis, [(i, i ^ apart) for i in range(size)])


def finish(own, received, gain):
    raw = own + received.astype(jnp.float32)
    raw_key = raw[:, :HD]
    scale = lax.rsqrt(jnp.mean(raw_key * raw_key, axis=-1, keepdims=True) + EPS)
    return (raw_key * scale * gain).astype(jnp.bfloat16), raw[:, HD:].astype(jnp.bfloat16)


def contract_last(left, right):
    return lax.dot_general(left, right, (((1,), (1,)), ((), ())), preferred_element_type=jnp.float32)


def attend(query_rows, old_keys, old_values, new_keys, new_values, old_seen, new_seen, out):
    rows = query_rows.shape[0]
    queries = jnp.concatenate([query_rows[:, h * HD : (h + 1) * HD] for h in range(QPK)], axis=0)
    scaling = HD ** (-0.5)
    old_scores = jnp.where(old_seen, contract_last(queries, old_keys) * scaling, MASKED_SCORE)
    new_scores = jnp.where(new_seen, contract_last(queries, new_keys) * scaling, MASKED_SCORE)
    highest = jnp.maximum(
        jnp.max(old_scores, axis=-1, keepdims=True), jnp.max(new_scores, axis=-1, keepdims=True)
    )
    old_exp = jnp.exp(old_scores - highest)
    new_exp = jnp.exp(new_scores - highest)
    totals = jnp.sum(old_exp, axis=-1, keepdims=True) + jnp.sum(new_exp, axis=-1, keepdims=True)
    old_prob = (old_exp / totals).astype(jnp.bfloat16)
    new_prob = (new_exp / totals).astype(jnp.bfloat16)
    blended = jnp.dot(old_prob, old_values, preferred_element_type=jnp.float32) + jnp.dot(
        new_prob, new_values, preferred_element_type=jnp.float32
    )
    blended = blended.astype(jnp.bfloat16)
    for h in range(QPK):
        out[:, h * HD : (h + 1) * HD] = blended[h * rows : (h + 1) * rows, :]


def new_mask(rows, steps, count, first):
    shape = (rows * QPK, count)
    step_bits = steps.bit_length() - 1
    row = (lax.broadcasted_iota(jnp.int32, shape, 0) & (rows - 1)) + first
    column = lax.broadcasted_iota(jnp.int32, shape, 1)
    return ((row >> step_bits) == (column >> step_bits)) & (column <= row)


def old_mask(rows, steps, owners, first):
    shape = (rows * QPK, owners.shape[1])
    step_bits = steps.bit_length() - 1
    row = (lax.broadcasted_iota(jnp.int32, shape, 0) & (rows - 1)) + first
    return (row >> step_bits) == owners


def pack_kernel(place, states, nexts, sequences, packed):
    next_rows = nexts[...].reshape(-1, packed.shape[1])
    sequence_rows = sequences[...].reshape(-1, packed.shape[1])
    fresh = next_rows.shape[0] + sequence_rows.shape[0]
    row = lax.broadcasted_iota(jnp.int32, (states.shape[0], place.shape[1]), 0)
    chooser = (row == place[...]).astype(jnp.float32).astype(jnp.bfloat16)
    live = jnp.dot(chooser, states[...], preferred_element_type=jnp.float32)
    packed[: next_rows.shape[0], :] = next_rows
    packed[next_rows.shape[0] : fresh, :] = sequence_rows
    packed[fresh:, :] = live.astype(jnp.bfloat16)


def pack(place, states, nexts, sequences):
    whole = pl.BlockSpec(memory_space=pltpu.VMEM)
    fresh = nexts.shape[0] * nexts.shape[1] + sequences.shape[0] * sequences.shape[1]
    rows = fresh + states.shape[0]
    return pl.pallas_call(
        pack_kernel,
        in_specs=[whole] * 4,
        out_specs=whole,
        out_shape=jax.ShapeDtypeStruct((rows, states.shape[1]), jnp.bfloat16),
        compiler_params=pltpu.CompilerParams(vmem_limit_bytes=24 * 2**20),
        name="pack",
    )(place, states, nexts, sequences)


def prompt_kernel(steps, own, got, gain, owners, query, out):
    fresh = own.shape[0] - owners.shape[1]
    count = query.shape[0]
    old_keys, old_values = finish(own[fresh:], got[fresh:], gain[...])
    new_keys, new_values = finish(own[:count], got[:count], gain[...])
    rows = GROUP * steps
    for first in range(0, count, rows):
        attend(
            query[first : first + rows],
            old_keys,
            old_values,
            new_keys[first : first + rows],
            new_values[first : first + rows],
            old_mask(rows, steps, owners[...], first),
            new_mask(rows, steps, rows, 0),
            out.at[pl.ds(first, rows)],
        )


def prompt_attention(own, got, gain, owners, query, steps):
    whole = pl.BlockSpec(memory_space=pltpu.VMEM)
    return pl.pallas_call(
        functools.partial(prompt_kernel, steps),
        in_specs=[whole] * 5,
        out_specs=whole,
        out_shape=jax.ShapeDtypeStruct(query.shape, jnp.bfloat16),
        compiler_params=pltpu.CompilerParams(vmem_limit_bytes=32 * 2**20),
        cost_estimate=pl.CostEstimate(flops=10**9, bytes_accessed=2 * 10**6, transcendentals=10**5),
        name="prompt_attention",
    )(own, got, gain, owners, query)


def cached_kernel(steps, own_new, got_new, gain, owners, query, cache, out):
    new_keys, new_values = finish(own_new[...], got_new[...], gain[...])
    sequences, _, context, _ = cache.shape
    old_keys = cache[:, 0].reshape(sequences * context, HD)
    old_values = cache[:, 1].reshape(sequences * context, HD)
    rows = query.shape[0]
    attend(
        query[...],
        old_keys,
        old_values,
        new_keys,
        new_values,
        old_mask(rows, steps, owners[...], 0),
        new_mask(rows, steps, rows, 0),
        out,
    )


def cached_attention(own, got, gain, owners, query, cache, steps, first):
    rows = query.shape[0]
    fresh = pl.BlockSpec((rows, 2 * HD), lambda g: (first // rows, 0))
    return pl.pallas_call(
        functools.partial(cached_kernel, steps),
        grid=(1,),
        in_specs=[
            fresh,
            fresh,
            pl.BlockSpec((1, HD), lambda g: (0, 0)),
            pl.BlockSpec(owners.shape, lambda g: (0, 0)),
            pl.BlockSpec(query.shape, lambda g: (0, 0)),
            pl.BlockSpec(cache.shape, lambda g: (0, 0, 0, 0)),
        ],
        out_specs=pl.BlockSpec(query.shape, lambda g: (0, 0)),
        out_shape=jax.ShapeDtypeStruct(query.shape, jnp.bfloat16),
        compiler_params=pltpu.CompilerParams(vmem_limit_bytes=24 * 2**20),
        cost_estimate=pl.CostEstimate(flops=10**9, bytes_accessed=2 * 10**6, transcendentals=10**5),
        name="cached_attention",
    )(own, got, gain, owners, query, cache)


def spread(share):
    copies = jnp.broadcast_to(share[None], (lax.axis_size("grp"),) + share.shape)
    arrived = lax.all_to_all(copies, "grp", split_axis=0, concat_axis=0, tiled=True)
    return arrived.reshape(-1, share.shape[1])


def multiply_kernel(count, order, block_number, *refs):
    features, weights, (begun, result, total) = refs[:count], refs[count:-3], refs[-3:]
    k = pl.program_id(0)

    @pl.when(k == 0)
    def _():
        total[...] = jnp.broadcast_to(begun[...], total.shape)

    def add(block):
        weight = jnp.concatenate([block_ref[...] for block_ref in weights], axis=1)
        total[...] += jnp.dot(block[...], weight, preferred_element_type=jnp.float32)

    for index, block in enumerate(features):
        pl.when(k == index)(functools.partial(add, block))

    @pl.when(k == pl.num_programs(0) - 1)
    def _():
        result[...] = total[...].astype(result.dtype)


def multiply(begun, features, order, block_number, weights, by_block, dtype):
    rows, width = features[0].shape
    columns = begun.shape[1]
    number = lambda o, b, k: b[k] if by_block else o[k]
    whole = lambda *shape: pl.BlockSpec(shape, lambda k, o, b: (0, 0))
    return pl.pallas_call(
        functools.partial(multiply_kernel, len(features)),
        grid_spec=pltpu.PrefetchScalarGridSpec(
            num_scalar_prefetch=2,
            grid=(len(features),),
            in_specs=[whole(rows, width)] * len(features)
            + [
                pl.BlockSpec((width, weight.shape[1]), lambda k, o, b: (number(o, b, k), 0))
                for weight in weights
            ]
            + [whole(rows if begun.shape[0] == rows else 1, columns)],
            out_specs=whole(rows, columns),
            scratch_shapes=[pltpu.VMEM((rows, columns), jnp.float32)],
        ),
        out_shape=jax.ShapeDtypeStruct((rows, columns), dtype),
        compiler_params=pltpu.CompilerParams(vmem_limit_bytes=24 * 2**20),
        cost_estimate=pl.CostEstimate(
            flops=2 * len(features) * rows * width * columns,
            bytes_accessed=2 * 10**6,
            transcendentals=0,
        ),
        name="multiply",
    )(order, block_number, *features, *weights, begun)


def pass_on(block, awaited, flops=0):
    anywhere = pl.BlockSpec(memory_space=pl.ANY)
    return pl.pallas_call(
        lambda block_ref, awaited_ref, out_ref: None,
        in_specs=[anywhere, anywhere],
        out_specs=anywhere,
        out_shape=jax.ShapeDtypeStruct(block.shape, block.dtype),
        input_output_aliases={0: 0},
        cost_estimate=pl.CostEstimate(flops=flops, bytes_accessed=flops // 300, transcendentals=0),
        name="pass_on",
    )(block, awaited)


def rank_within(targets):
    slot_total = targets.shape[0]
    same_target = targets[:, None] == targets[None, :]
    earlier = jnp.arange(slot_total)[None, :] < jnp.arange(slot_total)[:, None]
    return jnp.sum(same_target & earlier, axis=1)


def prepare(
    prompt_states, prompt_lengths, prompt_query, prompt_next, key_weight, value_weight, seq_next
):
    groups = lax.axis_size("grp")
    group_index = lax.axis_index("grp")
    lane = lax.axis_index("tp")
    prompts = prompt_query.shape[0]
    prompt_len = prompt_states.shape[0] // prompts
    width = prompt_next.shape[2]

    share = QUAD * width // groups
    start = ((lane ^ 4) // QUAD * QUAD) * width + group_index * share
    weight_share = jnp.concatenate(
        [
            lax.dynamic_slice_in_dim(key_weight, start, share, 0),
            lax.dynamic_slice_in_dim(value_weight, start, share, 0),
        ],
        axis=1,
    )
    instance = lax.axis_index("pool") * groups + group_index
    lengths = lax.dynamic_index_in_dim(prompt_lengths, instance, 0, keepdims=False)
    ends = jnp.cumsum(lengths)
    position = jnp.arange(prompt_len)[None, :]
    place = jnp.where(position < lengths[:, None], (ends - lengths)[:, None] + position, -1)
    place = place.reshape(1, prompts * prompt_len).astype(jnp.int32)
    packed = pack(place, prompt_states, prompt_next, seq_next)
    received_share = exchange(pass_on(weight_share, packed), "tp", 4)
    return received_share, ends, packed


def run(
    kept,
    received_share,
    ends,
    packed,
    prompt_target,
    prompt_query,
    key_weight,
    value_weight,
    key_gain,
    seq_query,
    cache_kv,
    context_lengths,
):
    groups = lax.axis_size("grp")
    pool_index = lax.axis_index("pool")
    group_index = lax.axis_index("grp")
    lane = lax.axis_index("tp")
    prompts = prompt_query.shape[0]
    seq_count, steps, query_width = seq_query.shape
    quad = QUAD
    gain = key_gain.reshape(1, HD)
    prompt_owners = jnp.sum(ends[:, None] <= jnp.arange(kept)[None, :], axis=0, dtype=jnp.int32)
    prompt_owners = prompt_owners.reshape(1, kept)
    context = cache_kv.shape[2]
    seq_owners = jnp.where(
        jnp.arange(context)[None, :] < context_lengths[:, None],
        jnp.arange(seq_count, dtype=jnp.int32)[:, None],
        seq_count,
    ).reshape(1, seq_count * context)

    query_rows = prompt_query.reshape(prompts * steps, query_width)
    mine = packed[: (prompts + seq_count) * steps + kept]
    partner_weight = spread(received_share)

    order = jnp.asarray([0, 1, 2, 3], jnp.int32) ^ (lane % quad)
    block_number = lane // quad * quad + order
    second = exchange(mine, "tp", 2)
    first = exchange(mine, "tp", 1)
    second = pass_on(second, first, 8000000000)
    third = exchange(second, "tp", 1)
    blank = jnp.zeros((1, 2 * HD), jnp.float32)
    near = (mine, first, second)
    begun = multiply(
        blank, near, order[:3], block_number[:3], [partner_weight], False, jnp.float32
    )
    sent = multiply(
        begun, [third], order[3:], block_number[3:], [partner_weight], False, jnp.bfloat16
    )
    got = exchange(sent, "tp", 4)
    own = multiply(
        blank,
        near + (third,),
        order,
        block_number,
        [key_weight, value_weight],
        True,
        jnp.float32,
    )
    result = prompt_attention(own, got, gain, prompt_owners, query_rows, steps)
    crossed = exchange(result, "pool", 1)
    seq_output = cached_attention(
        own,
        got,
        gain,
        seq_owners,
        seq_query.reshape(seq_count * steps, query_width),
        cache_kv,
        steps,
        prompts * steps,
    ).reshape(seq_count, steps, query_width)

    source = (pool_index ^ 1) * groups + group_index
    targets = lax.dynamic_index_in_dim(prompt_target[:, :, 0], source, 0, keepdims=False)
    places = targets * MOST + rank_within(targets)
    place_rows = (places[:, None] * steps + jnp.arange(steps)[None, :]).reshape(-1)
    chooser = (jnp.arange(groups * MOST * steps)[:, None] == place_rows[None, :]).astype(
        jnp.bfloat16
    )
    outgoing = jnp.dot(chooser, crossed, preferred_element_type=jnp.float32).astype(jnp.bfloat16)
    arrived = lax.all_to_all(outgoing, "grp", split_axis=0, concat_axis=0, tiled=True)
    return seq_output, arrived.reshape(1, groups * MOST, steps, query_width)


def on_device(
    prompt_states,
    prompt_lengths,
    prompt_target,
    prompt_query,
    prompt_next,
    key_weight,
    value_weight,
    key_gain,
    seq_query,
    seq_next,
    cache_kv,
    context_lengths,
):
    rows = prompt_states.shape[0]
    most = jnp.max(jnp.sum(prompt_lengths, axis=1))
    sizes = [size for size in BUCKETS if size < rows] + [rows]
    choice = sum((most > size).astype(jnp.int32) for size in sizes[:-1])
    prepared = prepare(
        prompt_states, prompt_lengths, prompt_query, prompt_next, key_weight, value_weight, seq_next
    )
    return lax.switch(
        choice,
        [functools.partial(run, size) for size in sizes],
        *prepared,
        prompt_target,
        prompt_query,
        key_weight,
        value_weight,
        key_gain,
        seq_query,
        cache_kv,
        context_lengths,
    )


def solution(mesh):
    return jax.shard_map(
        on_device,
        mesh=mesh,
        in_specs=(
            P(("pool", "grp"), "tp"),
            P(),
            P(),
            P(("pool", "grp"), None, "tp"),
            P(("pool", "grp"), None, "tp"),
            P(None, "tp"),
            P(None, "tp"),
            P(),
            P(("pool", "grp"), None, "tp"),
            P(("pool", "grp"), None, "tp"),
            P(("pool", "grp"), None, None, "tp"),
            P(("pool", "grp")),
        ),
        out_specs=(P(("pool", "grp"), None, "tp"), P(("pool", "grp"), None, None, "tp")),
        check_vma=False,
    )
```

```python
import functools

import jax
import jax.numpy as jnp
from jax import lax
from jax.experimental import pallas as pl
from jax.experimental.pallas import tpu as pltpu
from jax.sharding import PartitionSpec as P

HD = 128
QPK = 8
MOST = 2
EPS = 1e-06
MASKED_SCORE = -1e30
GROUP = 8
QUAD = 4
BUCKETS = (336, 352, 368, 384)


def exchange(block, axis, apart):
    size = lax.axis_size(axis)
    return lax.ppermute(block, axis, [(i, i ^ apart) for i in range(size)])


def finish(own, received, gain):
    raw = own + received.astype(jnp.float32)
    raw_key = raw[:, :HD]
    scale = lax.rsqrt(jnp.mean(raw_key * raw_key, axis=-1, keepdims=True) + EPS)
    return (raw_key * scale * gain).astype(jnp.bfloat16), raw[:, HD:].astype(jnp.bfloat16)


def contract_last(left, right):
    return lax.dot_general(left, right, (((1,), (1,)), ((), ())), preferred_element_type=jnp.float32)


def attend(query_rows, old_keys, old_values, new_keys, new_values, old_seen, new_seen, out):
    rows = query_rows.shape[0]
    queries = jnp.concatenate([query_rows[:, h * HD : (h + 1) * HD] for h in range(QPK)], axis=0)
    scaling = HD ** (-0.5)
    old_scores = jnp.where(old_seen, contract_last(queries, old_keys) * scaling, MASKED_SCORE)
    new_scores = jnp.where(new_seen, contract_last(queries, new_keys) * scaling, MASKED_SCORE)
    highest = jnp.maximum(
        jnp.max(old_scores, axis=-1, keepdims=True), jnp.max(new_scores, axis=-1, keepdims=True)
    )
    old_exp = jnp.exp(old_scores - highest)
    new_exp = jnp.exp(new_scores - highest)
    totals = jnp.sum(old_exp, axis=-1, keepdims=True) + jnp.sum(new_exp, axis=-1, keepdims=True)
    old_prob = (old_exp / totals).astype(jnp.bfloat16)
    new_prob = (new_exp / totals).astype(jnp.bfloat16)
    blended = jnp.dot(old_prob, old_values, preferred_element_type=jnp.float32) + jnp.dot(
        new_prob, new_values, preferred_element_type=jnp.float32
    )
    blended = blended.astype(jnp.bfloat16)
    for h in range(QPK):
        out[:, h * HD : (h + 1) * HD] = blended[h * rows : (h + 1) * rows, :]


def new_mask(rows, steps, count, first):
    shape = (rows * QPK, count)
    step_bits = steps.bit_length() - 1
    row = (lax.broadcasted_iota(jnp.int32, shape, 0) & (rows - 1)) + first
    column = lax.broadcasted_iota(jnp.int32, shape, 1)
    return ((row >> step_bits) == (column >> step_bits)) & (column <= row)


def old_mask(rows, steps, owners, first):
    shape = (rows * QPK, owners.shape[1])
    step_bits = steps.bit_length() - 1
    row = (lax.broadcasted_iota(jnp.int32, shape, 0) & (rows - 1)) + first
    return (row >> step_bits) == owners


def pack_kernel(prompt_len, instance, lengths, states, nexts, sequences, packed):
    here = lax.broadcasted_iota(jnp.int32, lengths.shape, 0) == instance[0]
    mine = jnp.sum(jnp.where(here, lengths[...], 0), axis=0, keepdims=True)
    mine = jnp.broadcast_to(mine.astype(jnp.float32), (8, mine.shape[1])).astype(jnp.bfloat16)
    shape = (lengths.shape[1], states.shape[0])
    prompt = lax.broadcasted_iota(jnp.int32, shape, 0)
    source = lax.broadcasted_iota(jnp.int32, shape, 1) // prompt_len

    def total(chosen):
        chosen = chosen.astype(jnp.float32).astype(jnp.bfloat16)
        sums = jnp.dot(mine, chosen, preferred_element_type=jnp.float32)
        return sums[:1].astype(jnp.int32)

    position = lax.broadcasted_iota(jnp.int32, (1, shape[1]), 1) % prompt_len
    place = jnp.where(
        position < total(prompt == source), total(prompt < source) + position, -1
    )
    next_rows = nexts[...].reshape(-1, packed.shape[1])
    sequence_rows = sequences[...].reshape(-1, packed.shape[1])
    fresh = next_rows.shape[0] + sequence_rows.shape[0]
    row = lax.broadcasted_iota(jnp.int32, (states.shape[0], shape[1]), 0)
    chooser = (row == place).astype(jnp.float32).astype(jnp.bfloat16)
    live = jnp.dot(chooser, states[...], preferred_element_type=jnp.float32)
    packed[: next_rows.shape[0], :] = next_rows
    packed[next_rows.shape[0] : fresh, :] = sequence_rows
    packed[fresh:, :] = live.astype(jnp.bfloat16)


def pack(instance, lengths, states, nexts, sequences):
    whole = pl.BlockSpec(memory_space=pltpu.VMEM)
    fresh = nexts.shape[0] * nexts.shape[1] + sequences.shape[0] * sequences.shape[1]
    rows = fresh + states.shape[0]
    return pl.pallas_call(
        functools.partial(pack_kernel, states.shape[0] // lengths.shape[1]),
        in_specs=[pl.BlockSpec(memory_space=pltpu.SMEM)] + [whole] * 4,
        out_specs=whole,
        out_shape=jax.ShapeDtypeStruct((rows, states.shape[1]), jnp.bfloat16),
        compiler_params=pltpu.CompilerParams(vmem_limit_bytes=60 * 2**20),
        name="pack",
    )(instance.reshape(1), lengths, states, nexts, sequences)


def prompt_kernel(steps, own, got, gain, owners, query, out):
    fresh = own.shape[0] - owners.shape[1]
    count = query.shape[0]
    old_keys, old_values = finish(own[fresh:], got[fresh:], gain[...])
    new_keys, new_values = finish(own[:count], got[:count], gain[...])
    rows = GROUP * steps
    for first in range(0, count, rows):
        attend(
            query[first : first + rows],
            old_keys,
            old_values,
            new_keys[first : first + rows],
            new_values[first : first + rows],
            old_mask(rows, steps, owners[...], first),
            new_mask(rows, steps, rows, 0),
            out.at[pl.ds(first, rows)],
        )


def prompt_attention(own, got, gain, owners, query, steps):
    whole = pl.BlockSpec(memory_space=pltpu.VMEM)
    return pl.pallas_call(
        functools.partial(prompt_kernel, steps),
        in_specs=[whole] * 5,
        out_specs=whole,
        out_shape=jax.ShapeDtypeStruct(query.shape, jnp.bfloat16),
        compiler_params=pltpu.CompilerParams(vmem_limit_bytes=32 * 2**20),
        cost_estimate=pl.CostEstimate(flops=10**9, bytes_accessed=2 * 10**6, transcendentals=10**5),
        name="prompt_attention",
    )(own, got, gain, owners, query)


def cached_kernel(steps, own_new, got_new, gain, owners, query, cache, out):
    new_keys, new_values = finish(own_new[...], got_new[...], gain[...])
    sequences, _, context, _ = cache.shape
    old_keys = cache[:, 0].reshape(sequences * context, HD)
    old_values = cache[:, 1].reshape(sequences * context, HD)
    rows = query.shape[0]
    attend(
        query[...],
        old_keys,
        old_values,
        new_keys,
        new_values,
        old_mask(rows, steps, owners[...], 0),
        new_mask(rows, steps, rows, 0),
        out,
    )


def cached_attention(own, got, gain, owners, query, cache, steps, first):
    rows = query.shape[0]
    fresh = pl.BlockSpec((rows, 2 * HD), lambda g: (first // rows, 0))
    return pl.pallas_call(
        functools.partial(cached_kernel, steps),
        grid=(1,),
        in_specs=[
            fresh,
            fresh,
            pl.BlockSpec((1, HD), lambda g: (0, 0)),
            pl.BlockSpec(owners.shape, lambda g: (0, 0)),
            pl.BlockSpec(query.shape, lambda g: (0, 0)),
            pl.BlockSpec(cache.shape, lambda g: (0, 0, 0, 0)),
        ],
        out_specs=pl.BlockSpec(query.shape, lambda g: (0, 0)),
        out_shape=jax.ShapeDtypeStruct(query.shape, jnp.bfloat16),
        compiler_params=pltpu.CompilerParams(vmem_limit_bytes=24 * 2**20),
        cost_estimate=pl.CostEstimate(flops=10**9, bytes_accessed=2 * 10**6, transcendentals=10**5),
        name="cached_attention",
    )(own, got, gain, owners, query, cache)


def spread(share):
    copies = jnp.broadcast_to(share[None], (lax.axis_size("grp"),) + share.shape)
    arrived = lax.all_to_all(copies, "grp", split_axis=0, concat_axis=0, tiled=True)
    return arrived.reshape(-1, share.shape[1])


def multiply_kernel(count, order, block_number, *refs):
    features, weights, (begun, result, total) = refs[:count], refs[count:-3], refs[-3:]
    k = pl.program_id(0)

    @pl.when(k == 0)
    def _():
        total[...] = jnp.broadcast_to(begun[...], total.shape)

    def add(block):
        weight = jnp.concatenate([block_ref[...] for block_ref in weights], axis=1)
        total[...] += jnp.dot(block[...], weight, preferred_element_type=jnp.float32)

    for index, block in enumerate(features):
        pl.when(k == index)(functools.partial(add, block))

    @pl.when(k == pl.num_programs(0) - 1)
    def _():
        result[...] = total[...].astype(result.dtype)


def multiply(begun, features, order, block_number, weights, by_block, dtype):
    rows, width = features[0].shape
    columns = begun.shape[1]
    number = lambda o, b, k: b[k] if by_block else o[k]
    whole = lambda *shape: pl.BlockSpec(shape, lambda k, o, b: (0, 0))
    return pl.pallas_call(
        functools.partial(multiply_kernel, len(features)),
        grid_spec=pltpu.PrefetchScalarGridSpec(
            num_scalar_prefetch=2,
            grid=(len(features),),
            in_specs=[whole(rows, width)] * len(features)
            + [
                pl.BlockSpec((width, weight.shape[1]), lambda k, o, b: (number(o, b, k), 0))
                for weight in weights
            ]
            + [whole(rows if begun.shape[0] == rows else 1, columns)],
            out_specs=whole(rows, columns),
            scratch_shapes=[pltpu.VMEM((rows, columns), jnp.float32)],
        ),
        out_shape=jax.ShapeDtypeStruct((rows, columns), dtype),
        compiler_params=pltpu.CompilerParams(vmem_limit_bytes=24 * 2**20),
        cost_estimate=pl.CostEstimate(
            flops=2 * len(features) * rows * width * columns,
            bytes_accessed=2 * 10**6,
            transcendentals=0,
        ),
        name="multiply",
    )(order, block_number, *features, *weights, begun)


def pass_on(block, awaited, flops=0):
    anywhere = pl.BlockSpec(memory_space=pl.ANY)
    return pl.pallas_call(
        lambda block_ref, awaited_ref, out_ref: None,
        in_specs=[anywhere, anywhere],
        out_specs=anywhere,
        out_shape=jax.ShapeDtypeStruct(block.shape, block.dtype),
        input_output_aliases={0: 0},
        cost_estimate=pl.CostEstimate(flops=flops, bytes_accessed=flops // 300, transcendentals=0),
        name="pass_on",
    )(block, awaited)


def rank_within(targets):
    slot_total = targets.shape[0]
    same_target = targets[:, None] == targets[None, :]
    earlier = jnp.arange(slot_total)[None, :] < jnp.arange(slot_total)[:, None]
    return jnp.sum(same_target & earlier, axis=1)


def prepare(
    prompt_states, prompt_lengths, prompt_next, key_weight, value_weight, seq_next
):
    groups = lax.axis_size("grp")
    group_index = lax.axis_index("grp")
    lane = lax.axis_index("tp")
    width = prompt_next.shape[2]

    share = QUAD * width // groups
    start = ((lane ^ 4) // QUAD * QUAD) * width + group_index * share
    weight_share = jnp.concatenate(
        [
            lax.dynamic_slice_in_dim(key_weight, start, share, 0),
            lax.dynamic_slice_in_dim(value_weight, start, share, 0),
        ],
        axis=1,
    )
    instance = lax.axis_index("pool") * groups + group_index
    lengths = lax.dynamic_index_in_dim(prompt_lengths, instance, 0, keepdims=False)
    ends = jnp.cumsum(lengths)
    packed = pack(instance, prompt_lengths, prompt_states, prompt_next, seq_next)
    received_share = exchange(pass_on(weight_share, packed), "tp", 4)
    return received_share, ends, packed


def run(
    kept,
    received_share,
    ends,
    packed,
    prompt_target,
    prompt_query,
    key_weight,
    value_weight,
    key_gain,
    seq_query,
    cache_kv,
    context_lengths,
):
    groups = lax.axis_size("grp")
    pool_index = lax.axis_index("pool")
    group_index = lax.axis_index("grp")
    lane = lax.axis_index("tp")
    prompts = prompt_query.shape[0]
    seq_count, steps, query_width = seq_query.shape
    quad = QUAD
    gain = key_gain.reshape(1, HD)
    prompt_owners = jnp.sum(ends[:, None] <= jnp.arange(kept)[None, :], axis=0, dtype=jnp.int32)
    prompt_owners = prompt_owners.reshape(1, kept)
    context = cache_kv.shape[2]
    seq_owners = jnp.where(
        jnp.arange(context)[None, :] < context_lengths[:, None],
        jnp.arange(seq_count, dtype=jnp.int32)[:, None],
        seq_count,
    ).reshape(1, seq_count * context)

    query_rows = prompt_query.reshape(prompts * steps, query_width)
    mine = packed[: (prompts + seq_count) * steps + kept]
    partner_weight = spread(received_share)

    order = jnp.asarray([0, 1, 2, 3], jnp.int32) ^ (lane % quad)
    block_number = lane // quad * quad + order
    second = exchange(mine, "tp", 2)
    first = exchange(mine, "tp", 1)
    second = pass_on(second, first, 8000000000)
    third = exchange(second, "tp", 1)
    blank = jnp.zeros((1, 2 * HD), jnp.float32)
    near = (mine, first, second)
    begun = multiply(
        blank, near, order[:3], block_number[:3], [partner_weight], False, jnp.float32
    )
    sent = multiply(
        begun, [third], order[3:], block_number[3:], [partner_weight], False, jnp.bfloat16
    )
    got = exchange(sent, "tp", 4)
    own = multiply(
        blank,
        near + (third,),
        order,
        block_number,
        [key_weight, value_weight],
        True,
        jnp.float32,
    )
    result = prompt_attention(own, got, gain, prompt_owners, query_rows, steps)
    crossed = exchange(result, "pool", 1)
    seq_output = cached_attention(
        own,
        got,
        gain,
        seq_owners,
        seq_query.reshape(seq_count * steps, query_width),
        cache_kv,
        steps,
        prompts * steps,
    ).reshape(seq_count, steps, query_width)

    source = (pool_index ^ 1) * groups + group_index
    targets = lax.dynamic_index_in_dim(prompt_target[:, :, 0], source, 0, keepdims=False)
    places = targets * MOST + rank_within(targets)
    place_rows = (places[:, None] * steps + jnp.arange(steps)[None, :]).reshape(-1)
    chooser = (jnp.arange(groups * MOST * steps)[:, None] == place_rows[None, :]).astype(
        jnp.bfloat16
    )
    outgoing = jnp.dot(chooser, crossed, preferred_element_type=jnp.float32).astype(jnp.bfloat16)
    arrived = lax.all_to_all(outgoing, "grp", split_axis=0, concat_axis=0, tiled=True)
    return seq_output, arrived.reshape(1, groups * MOST, steps, query_width)


def on_device(
    prompt_states,
    prompt_lengths,
    prompt_target,
    prompt_query,
    prompt_next,
    key_weight,
    value_weight,
    key_gain,
    seq_query,
    seq_next,
    cache_kv,
    context_lengths,
):
    rows = prompt_states.shape[0]
    most = jnp.max(jnp.sum(prompt_lengths, axis=1))
    sizes = [size for size in BUCKETS if size < rows] + [rows]
    choice = sum((most > size).astype(jnp.int32) for size in sizes[:-1])
    prepared = prepare(
        prompt_states, prompt_lengths, prompt_next, key_weight, value_weight, seq_next
    )
    return lax.switch(
        choice,
        [functools.partial(run, size) for size in sizes],
        *prepared,
        prompt_target,
        prompt_query,
        key_weight,
        value_weight,
        key_gain,
        seq_query,
        cache_kv,
        context_lengths,
    )


def solution(mesh):
    return jax.shard_map(
        on_device,
        mesh=mesh,
        in_specs=(
            P(("pool", "grp"), "tp"),
            P(),
            P(),
            P(("pool", "grp"), None, "tp"),
            P(("pool", "grp"), None, "tp"),
            P(None, "tp"),
            P(None, "tp"),
            P(),
            P(("pool", "grp"), None, "tp"),
            P(("pool", "grp"), None, "tp"),
            P(("pool", "grp"), None, None, "tp"),
            P(("pool", "grp")),
        ),
        out_specs=(P(("pool", "grp"), None, "tp"), P(("pool", "grp"), None, None, "tp")),
        check_vma=False,
    )
```
